1024 devices in a mesh: pair: 128 (over y, z), red: 8 (over x, core).
Axes of the slice: x: 4, y: 4, z: 32, core: 2. Of those that a mesh axis runs over, the one named last changes fastest.
Arguments:
- amplitudes: bfloat16 [1024, 8, 16, 64, 128], P('pair', 'red'), may hold values from -6 to 6
- integrals: bfloat16 [128, 8, 128, 128], P('pair', 'red'), may hold values from -0.09375 to 0.09375
- amp_mask: int32 [1024, 8, 16], P('pair', 'red'), may hold values 0 or 1
- kept_slab_indicator: int32 [128, 8], P('pair', 'red'), may hold values 0 or 1
Outputs:
- residual: bfloat16 [1024, 64, 1024], P('pair', 'red')
The draws below stay inside these ranges and needn't reach their ends.
All inputs are finite; a program needn't handle non-finite values. No bound on the sum of `amp_mask` or of `kept_slab_indicator` on one device may be relied on, other than what follows from the above.
Results may differ from the reference program's by a relative error of at most 0.017.
Values may be sent and summed in bfloat16 or wider, within the bound.
A program may use at most 32 MiB of HBM per device.

```python
import jax
import jax.numpy as jnp

OT = 64
VT = 128
NB = 8
PAIRS = 1024
CDQ = 16
CDR = 8
TILES = 128


def touch_ends(entries, own_key, least, top_value):
    spot = [jax.random.randint(jax.random.fold_in(own_key, axis), (), 0, length) for axis, length in enumerate(entries.shape)]
    widest = entries.shape.index(max(entries.shape))
    next_to = spot[:widest] + [(spot[widest] + 1) % entries.shape[widest]] + spot[widest + 1:]
    return entries.at[tuple(spot)].set(least).at[tuple(next_to)].set(top_value)


def block_levels(key, shape, shards, smallest, largest):
    level, own = 1.0, jax.random.fold_in(key, 6)
    for axis_at, blocks in shards:
        steps = jnp.exp(jax.random.uniform(jax.random.fold_in(own, axis_at), (blocks,), jnp.float32, smallest / len(shards), largest / len(shards)))
        level = level * jnp.repeat(steps, shape[axis_at] // blocks).reshape([-1 if axis == axis_at else 1 for axis in range(len(shape))])
    return level


def scatter_about(stream_key, extent, width, reach, pieces=(), kind=jnp.bfloat16):
    values = width * jax.random.normal(stream_key, extent, jnp.float32)
    if pieces:
        values = values * block_levels(stream_key, extent, pieces, -0.22, 0.18)
    return jnp.clip(values, -reach, reach).astype(kind)


def setup_inputs(seed: int = 0) -> dict:
    splits = jax.random.split(jax.random.key(seed), 5)
    return {
        "amplitudes": scatter_about(splits[0], (PAIRS, CDR, CDQ, OT, VT), 1.0, 6.0, ((0, 128), (1, 8))),
        "integrals": scatter_about(splits[1], (TILES, CDR, VT, VT), (VT * CDQ * CDR // 4) ** -0.5, 0.09375, ((0, 128), (1, 8))),
        "amp_mask": touch_ends((jax.random.randint(splits[2], (PAIRS, CDR, CDQ), 0, 2) < 1).astype(jnp.int32), jax.random.fold_in(splits[2], 1), 0, 1),
        "kept_slab_indicator": touch_ends((jax.random.randint(splits[3], (TILES, CDR), 0, 2) < 1).astype(jnp.int32), jax.random.fold_in(splits[3], 1), 0, 1),
    }


def reference(amplitudes, integrals, amp_mask, kept_slab_indicator):
    total = jnp.zeros((PAIRS * OT, NB * VT), jnp.float32)
    for share in range(CDR):
        masked_amplitudes = amplitudes[:, share] * amp_mask[:, share, :, None, None].astype(jnp.bfloat16)
        rows_mat = jnp.transpose(masked_amplitudes, (0, 2, 1, 3)).reshape(PAIRS * OT, CDQ * VT)
        weight = kept_slab_indicator[:, share].astype(jnp.bfloat16)
        scaled_contribution = integrals[:, share] * weight[:, None, None]
        ladder = jnp.transpose(scaled_contribution.reshape(NB, CDQ, VT, VT), (1, 2, 0, 3)).reshape(CDQ * VT, NB * VT)
        partial_value = jnp.dot(rows_mat, ladder, preferred_element_type=jnp.float32).astype(jnp.bfloat16)
        total = total + partial_value.astype(jnp.float32)
    return total.reshape(PAIRS, OT, NB * VT).astype(jnp.bfloat16)
```

```python
import functools

import jax
import jax.numpy as jnp
from jax import lax
from jax.experimental import pallas as pl
from jax.experimental.pallas import tpu as pltpu
from jax.sharding import PartitionSpec as P

MESH = pl.DeviceIdType.MESH
NY, NZ = 4, 32
PARTS = 2
EDGES = (
    (31, 0), (64, 0), (95, 31), (30, 31), (1, 0), (24, 0), (93, 95), (28, 30), (72, 64), (20, 24), (5, 1), (124, 28),
    (91, 93), (22, 24), (40, 72), (74, 72), (2, 1), (6, 5), (123, 124), (90, 91), (21, 22), (16, 20), (18, 20),
    (27, 123), (41, 40), (3, 2), (7, 6), (69, 5), (106, 74), (76, 74), (116, 20), (118, 22), (120, 24), (58, 90),
    (53, 21), (50, 18), (59, 27), (10, 106), (14, 16), (26, 58), (99, 3), (39, 7), (42, 41), (78, 74), (112, 16),
    (114, 18), (84, 116), (86, 118), (15, 16), (17, 18), (19, 20), (23, 24), (96, 0), (34, 2), (68, 69), (102, 6),
    (104, 72), (73, 74), (44, 76), (77, 76), (85, 53), (121, 120), (92, 124), (94, 30), (4, 3), (8, 104), (9, 41),
    (11, 10), (12, 44), (13, 14), (25, 26), (29, 28), (32, 96), (33, 1), (97, 1), (65, 1), (98, 2), (66, 34), (35, 3),
    (67, 99), (36, 68), (100, 99), (37, 5), (101, 5), (38, 39), (70, 102), (103, 7), (71, 39), (105, 73), (43, 42),
    (107, 106), (75, 76), (108, 76), (45, 77), (109, 77), (46, 78), (110, 78), (47, 15), (111, 112), (79, 78),
    (48, 50), (80, 112), (49, 50), (113, 114), (81, 17), (82, 50), (51, 19), (115, 116), (83, 84), (52, 20),
    (117, 85), (54, 22), (55, 23), (119, 120), (87, 86), (56, 24), (88, 24), (57, 59), (89, 121), (122, 123),
    (60, 92), (61, 93), (125, 93), (62, 94), (126, 30), (63, 95), (127, 95),
)
ORDER = (
    (0, 31), (1, 1), (1, 31), (0, 1), (1, 32), (0, 96), (0, 64), (1, 64), (0, 30), (1, 2), (1, 127), (1, 30), (0, 2),
    (0, 97), (1, 63), (0, 95), (1, 65), (0, 33), (0, 24), (1, 8), (1, 27), (1, 95), (0, 5), (0, 65), (1, 96),
    (0, 126), (1, 34), (0, 32), (1, 29), (0, 34), (0, 3), (0, 28), (1, 4), (0, 94), (1, 62), (1, 126), (1, 66),
    (0, 127), (0, 98), (1, 97), (0, 63), (0, 93), (1, 33), (1, 67), (1, 40), (0, 120), (0, 56), (0, 23), (1, 9),
    (0, 22), (1, 104), (1, 10), (1, 59), (1, 26), (0, 6), (1, 123), (1, 91), (0, 37), (1, 88), (0, 72), (0, 101),
    (1, 28), (0, 88), (0, 4), (1, 61), (1, 3), (0, 69), (0, 29), (0, 99), (1, 36), (1, 72), (0, 124), (0, 66),
    (0, 20), (1, 12), (1, 125), (0, 35), (0, 62), (1, 98), (1, 39), (1, 94), (0, 125), (1, 41), (0, 61), (1, 69),
    (1, 99), (0, 119), (0, 121), (0, 91), (1, 35), (0, 55), (0, 21), (1, 11), (1, 105), (1, 42), (1, 25), (0, 7),
    (0, 118), (0, 54), (1, 92), (1, 106), (1, 58), (0, 102), (1, 120), (1, 60), (0, 40), (0, 104), (1, 86), (1, 37),
    (0, 68), (1, 56), (0, 74), (1, 93), (0, 100), (0, 123), (0, 67), (1, 68), (0, 92), (1, 44), (0, 116), (0, 52),
    (1, 13), (0, 19), (1, 108), (1, 71), (0, 89), (0, 53), (1, 107), (1, 70), (1, 74), (0, 90), (1, 121), (1, 14),
    (0, 18), (0, 39), (0, 103), (1, 57), (0, 86), (1, 124), (1, 119), (0, 70), (0, 41), (1, 90), (1, 54), (1, 87),
    (0, 106), (1, 5), (0, 8), (1, 16), (0, 36), (0, 16), (0, 27), (0, 73), (1, 24), (1, 84), (1, 38), (1, 100),
    (0, 60), (1, 76), (0, 122), (0, 84), (1, 45), (0, 51), (0, 115), (0, 76), (1, 109), (0, 85), (1, 75), (1, 102),
    (0, 58), (1, 15), (0, 50), (0, 17), (1, 110), (1, 46), (1, 73), (0, 114), (1, 122), (0, 71), (0, 38), (1, 89),
    (0, 87), (1, 23), (1, 118), (0, 9), (1, 82), (0, 42), (0, 10), (1, 53), (1, 22), (0, 107), (1, 48), (0, 78),
    (1, 55), (0, 59), (0, 15), (1, 101), (1, 17), (0, 105), (0, 112), (1, 85), (1, 116), (1, 83), (1, 52), (0, 14),
    (0, 108), (0, 83), (0, 44), (1, 77), (0, 117), (0, 75), (1, 18), (1, 43), (0, 77), (1, 6), (0, 26), (1, 78),
    (0, 49), (1, 111), (0, 82), (1, 47), (0, 113), (0, 48), (1, 50), (1, 117), (0, 43), (1, 81), (1, 112), (1, 79),
    (0, 46), (0, 11), (1, 114), (1, 21), (0, 81), (1, 49), (1, 80), (1, 113), (0, 79), (0, 110), (0, 80), (0, 111),
    (0, 47), (1, 51), (1, 20), (0, 12), (0, 13), (0, 57), (1, 19), (1, 115), (0, 45), (1, 103), (0, 25), (1, 7),
    (0, 109),
)


def split(code):
    return code // NZ, code % NZ


def mirrored(code):
    oy, oz = split(code)
    return (-oy % NY) * NZ + -oz % NZ


def plan():
    children = {}
    for child, parent in EDGES:
        for part in range(PARTS):
            turn = mirrored if part % 2 else (lambda code: code)
            children.setdefault((part, turn(parent)), []).append(turn(child))
    return children


def kernel(
    red, amp_ref, int_ref, mask_ref, kept_ref, out_ref,
    raw, lhs, tiles, total, part, landed,
    amp_sem, send_sem, recv_sem, red_send, red_recv,
):
    pair, me = lax.axis_index("pair"), lax.axis_index("red")
    y, z = lax.div(pair, NZ), lax.rem(pair, NZ)
    children = plan()
    step = tiles.shape[2] // PARTS
    pairs, slabs, occ, width = raw.shape
    group = 2 * width

    def at(oy, oz):
        return lax.rem(y + (oy % NY), NY), lax.rem(z + (oz % NZ), NZ)

    def chip(oy, oz):
        ny, nz = at(oy, oz)
        return (ny * NZ + nz, me)

    def copy(piece, child, parent):
        cy, cz = split(child)
        py, pz = split(parent)
        sy, sz = at(-py, -pz)
        slot = tiles.at[sy, sz, pl.ds(piece * step, step)]
        return pltpu.make_async_remote_copy(
            src_ref=slot, dst_ref=slot,
            send_sem=send_sem.at[piece * NY * NZ + child],
            recv_sem=recv_sem.at[piece * NY * NZ + child],
            device_id=chip(cy - py, cz - pz), device_id_type=MESH,
        )

    load = pltpu.make_async_copy(amp_ref.at[:, 0], raw, amp_sem)
    load.start()

    hops = set()
    for (piece, parent), below in children.items():
        for child in below:
            (cy, cz), (py, pz) = split(child), split(parent)
            hop = ((cy - py) % NY, (cz - pz) % NZ)
            hops |= {hop, (-hop[0] % NY, -hop[1] % NZ)}
    hops = sorted(hops)
    barrier = pltpu.get_barrier_semaphore()
    for hop in hops:
        pl.semaphore_signal(barrier, 1, device_id=chip(*hop), device_id_type=MESH)
    for d in range(1, red):
        pl.semaphore_signal(barrier, 1, device_id=(pair, lax.rem(me + d, red)), device_id_type=MESH)

    kept = kept_ref[0, 0].astype(jnp.float32)
    tiles[y, z] = (int_ref[0, 0].astype(jnp.float32) * kept).astype(jnp.bfloat16)
    pl.semaphore_wait(barrier, len(hops) + red - 1)

    def forward(piece, code):
        for child in children.get((piece, code), ()):
            copy(piece, child, code).start()

    for piece in range(PARTS):
        forward(piece, 0)

    load.wait()

    @pl.loop(0, pairs)
    def _(p):
        rows = pl.ds(pl.multiple_of(p * occ, occ), occ)
        for k in range(slabs):
            weight = mask_ref[p, 0, k].astype(jnp.float32).astype(jnp.bfloat16)
            lhs[rows, k * width:(k + 1) * width] = raw[p, k] * weight

    def red_copy(g, d):
        owner = lax.rem(me + d, red)
        return pltpu.make_async_remote_copy(
            src_ref=part.at[g, owner], dst_ref=landed.at[g, me],
            send_sem=red_send.at[g, d], recv_sem=red_recv.at[g, d],
            device_id=(pair, owner), device_id_type=MESH,
        )

    def multiply(g):
        column, _ = at(-g, 0)
        rhs = jnp.concatenate(
            [tiles[column, h * slabs:(h + 1) * slabs].reshape(slabs * width, width) for h in range(2)], axis=1
        )
        total[...] = jnp.dot(lhs[...], rhs, preferred_element_type=jnp.float32)
        low = occ // red
        for j in range(red):
            rows = [total[p * occ + j * low:p * occ + (j + 1) * low, :] for p in range(pairs)]
            part[g, j] = jnp.concatenate(rows, axis=0).astype(jnp.bfloat16)
        for d in range(1, red):
            red_copy(g, d).start()

    def finish(g):
        column, _ = at(-g, 0)
        value = part[g, me].astype(jnp.float32)
        for d in range(1, red):
            red_copy(g, d).wait_recv()
            value = value + landed[g, lax.rem(me + red - d, red)].astype(jnp.float32)
        spot = pl.ds(pl.multiple_of(column * group, group), group)
        out_ref[:, :, spot] = value.reshape(pairs, occ // red, group).astype(jnp.bfloat16)

    missing = {g: PARTS * NZ for g in range(NY)}
    missing[0] -= PARTS
    done = []
    for piece, code in ORDER:
        copy(piece, code, code).wait_recv()
        forward(piece, code)
        g = code // NZ
        missing[g] -= 1
        if missing[g] == 0:
            multiply(g)
            done.append(g)
            if len(done) > 1:
                finish(done[-2])
    finish(done[-1])

    for (piece, parent), below in children.items():
        for child in below:
            copy(piece, child, parent).wait_send()
    for g in range(NY):
        for d in range(1, red):
            red_copy(g, d).wait_send()


def local(red, amplitudes, integrals, amp_mask, kept_slab_indicator):
    pairs, _, slabs, occ, width = amplitudes.shape
    rows, group = pairs * occ, 2 * width
    out = jax.ShapeDtypeStruct((pairs, occ // red, NY * group), jnp.bfloat16)
    dma = pltpu.SemaphoreType.DMA
    return pl.pallas_call(
        functools.partial(kernel, red),
        out_shape=out,
        in_specs=[
            pl.BlockSpec(memory_space=pl.ANY),
            pl.BlockSpec(memory_space=pltpu.VMEM),
            pl.BlockSpec(memory_space=pltpu.SMEM),
            pl.BlockSpec(memory_space=pltpu.SMEM),
        ],
        out_specs=pl.BlockSpec(memory_space=pltpu.VMEM),
        scratch_shapes=[
            pltpu.VMEM((pairs, slabs, occ, width), jnp.bfloat16),
            pltpu.VMEM((rows, slabs * width), jnp.bfloat16),
            pltpu.VMEM((NY, NZ, width, width), jnp.bfloat16),
            pltpu.VMEM((rows, group), jnp.float32),
            pltpu.VMEM((NY, red, rows // red, group), jnp.bfloat16),
            pltpu.VMEM((NY, red, rows // red, group), jnp.bfloat16),
            dma, dma((PARTS * NY * NZ,)), dma((PARTS * NY * NZ,)), dma((NY, red)), dma((NY, red)),
        ],
        compiler_params=pltpu.CompilerParams(
            collective_id=0, has_side_effects=True, vmem_limit_bytes=48 * 1024 * 1024
        ),
    )(amplitudes, integrals, amp_mask, kept_slab_indicator)


def solution(mesh):
    return jax.shard_map(
        functools.partial(local, mesh.shape["red"]),
        mesh=mesh,
        in_specs=(
            P("pair", "red", None, None, None),
            P("pair", "red", None, None),
            P("pair", "red", None),
            P("pair", "red"),
        ),
        out_specs=P("pair", "red", None),
        check_vma=False,
    )
```

```python
import functools

import jax
import jax.numpy as jnp
from jax import lax
from jax.experimental import pallas as pl
from jax.experimental.pallas import tpu as pltpu
from jax.sharding import PartitionSpec as P

MESH = pl.DeviceIdType.MESH
NY, NZ = 4, 32
EDGES = (
    (25, 0), (1, 0), (31, 0), (9, 1), (29, 31), (3, 0), (24, 25), (61, 29), (18, 25), (23, 24), (5, 3), (10, 9),
    (60, 61), (12, 9), (21, 23), (6, 5), (33, 1), (41, 9), (55, 23), (59, 60), (106, 10), (127, 31), (15, 12),
    (13, 12), (114, 18), (4, 3), (7, 6), (17, 18), (19, 18), (20, 21), (27, 59), (34, 33), (54, 55), (57, 25),
    (73, 41), (74, 106), (93, 61), (101, 5), (119, 23), (121, 25), (126, 127), (14, 13), (82, 114), (108, 12),
    (2, 34), (11, 10), (16, 17), (36, 4), (38, 6), (40, 41), (45, 13), (47, 15), (49, 17), (51, 19), (56, 24),
    (58, 57), (72, 73), (75, 74), (86, 54), (92, 93), (94, 126), (102, 101), (103, 7), (113, 17), (116, 20),
    (118, 119), (122, 121), (123, 27), (64, 0), (65, 1), (67, 3), (78, 14), (80, 82), (95, 31), (110, 108), (8, 40),
    (22, 23), (26, 122), (28, 29), (30, 29), (32, 0), (35, 3), (37, 38), (39, 40), (42, 74), (43, 11), (44, 12),
    (46, 14), (48, 16), (50, 49), (52, 51), (53, 54), (62, 94), (63, 31), (66, 34), (68, 36), (69, 101), (70, 102),
    (71, 72), (76, 75), (77, 45), (79, 47), (81, 82), (83, 51), (84, 116), (85, 86), (87, 86), (88, 56), (89, 121),
    (90, 58), (91, 123), (96, 0), (97, 1), (98, 2), (99, 3), (100, 4), (104, 103), (105, 9), (107, 108), (109, 13),
    (111, 15), (112, 113), (115, 114), (117, 118), (120, 24), (124, 92), (125, 29),
)
ORDER = (
    (0, 1), (1, 31), (0, 96), (1, 32), (0, 31), (1, 1), (0, 32), (1, 96), (0, 64), (1, 64), (0, 3), (1, 29), (0, 33),
    (1, 127), (0, 97), (1, 63), (0, 127), (1, 33), (0, 29), (1, 3), (0, 63), (1, 97), (0, 25), (1, 7), (0, 65),
    (1, 95), (0, 95), (1, 65), (0, 99), (1, 61), (0, 4), (1, 28), (0, 35), (1, 125), (0, 67), (1, 93), (0, 34),
    (1, 126), (0, 5), (1, 27), (0, 126), (1, 34), (0, 61), (1, 99), (0, 30), (1, 2), (0, 125), (1, 35), (0, 28),
    (1, 4), (0, 24), (1, 8), (0, 121), (1, 39), (0, 57), (1, 103), (0, 9), (1, 23), (0, 36), (1, 124), (0, 100),
    (1, 60), (0, 2), (1, 30), (0, 6), (1, 26), (0, 66), (1, 94), (0, 101), (1, 59), (0, 60), (1, 100), (0, 94),
    (1, 66), (0, 93), (1, 67), (0, 23), (1, 9), (0, 56), (1, 104), (0, 122), (1, 38), (0, 120), (1, 40), (0, 58),
    (1, 102), (0, 89), (1, 71), (0, 10), (1, 22), (0, 41), (1, 119), (0, 105), (1, 55), (0, 18), (1, 14), (0, 68),
    (1, 92), (0, 98), (1, 62), (0, 7), (1, 25), (0, 38), (1, 122), (0, 102), (1, 58), (0, 69), (1, 91), (0, 12),
    (1, 20), (0, 59), (1, 101), (0, 62), (1, 98), (0, 92), (1, 68), (0, 55), (1, 105), (0, 119), (1, 41), (0, 22),
    (1, 10), (0, 88), (1, 72), (0, 26), (1, 6), (0, 11), (1, 21), (0, 21), (1, 11), (0, 90), (1, 70), (0, 40),
    (1, 120), (0, 106), (1, 54), (0, 17), (1, 15), (0, 73), (1, 87), (0, 19), (1, 13), (0, 114), (1, 46), (0, 37),
    (1, 123), (0, 103), (1, 57), (0, 70), (1, 90), (0, 13), (1, 19), (0, 108), (1, 52), (0, 44), (1, 116), (0, 54),
    (1, 106), (0, 27), (1, 5), (0, 124), (1, 36), (0, 118), (1, 42), (0, 43), (1, 117), (0, 20), (1, 12), (0, 15),
    (1, 17), (0, 8), (1, 24), (0, 39), (1, 121), (0, 74), (1, 86), (0, 16), (1, 16), (0, 113), (1, 47), (0, 72),
    (1, 88), (0, 49), (1, 111), (0, 115), (1, 45), (0, 51), (1, 109), (0, 104), (1, 56), (0, 82), (1, 78), (0, 14),
    (1, 18), (0, 45), (1, 115), (0, 109), (1, 51), (0, 107), (1, 53), (0, 86), (1, 74), (0, 123), (1, 37), (0, 53),
    (1, 107), (0, 110), (1, 50), (0, 116), (1, 44), (0, 117), (1, 43), (0, 47), (1, 113), (0, 75), (1, 85), (0, 111),
    (1, 49), (0, 112), (1, 48), (0, 42), (1, 118), (0, 71), (1, 89), (0, 48), (1, 112), (0, 50), (1, 110), (0, 83),
    (1, 77), (0, 52), (1, 108), (0, 46), (1, 114), (0, 81), (1, 79), (0, 77), (1, 83), (0, 87), (1, 73), (0, 80),
    (1, 80), (0, 91), (1, 69), (0, 78), (1, 82), (0, 85), (1, 75), (0, 84), (1, 76), (0, 79), (1, 81), (0, 76),
    (1, 84),
)
COLUMNS = (0, 1, 3, 2)


def split(code):
    return code // NZ, code % NZ


def mirrored(code):
    oy, oz = split(code)
    return (-oy % NY) * NZ + -oz % NZ


def plan():
    children = {}
    for child, parent in EDGES:
        children.setdefault((0, parent), []).append(child)
        children.setdefault((1, mirrored(parent)), []).append(mirrored(child))
    return children


def kernel(
    red, amp_ref, int_ref, mask_ref, kept_ref, out_ref,
    raw, lhs, own, mask, flag, tiles, total, part, met, pooled, landed,
    load_sem, send_sem, recv_sem, met_send, met_recv, red_send, red_recv,
):
    pair, me = lax.axis_index("pair"), lax.axis_index("red")
    y, z = lax.div(pair, NZ), lax.rem(pair, NZ)
    children = plan()
    inner = [node for node in ((0, 0), (1, 0)) + ORDER if node in children]
    sem_of = {node: NY + i for i, node in enumerate(inner)}
    pairs, slabs, occ, width = raw.shape
    group = 2 * width

    def at(oy, oz):
        return lax.rem(y + (oy % NY), NY), lax.rem(z + (oz % NZ), NZ)

    def chip(oy, oz):
        ny, nz = at(oy, oz)
        return (ny * NZ + nz, me)

    def copy(half, child, parent):
        cy, cz = split(child)
        py, pz = split(parent)
        sy, sz = at(-py, -pz)
        slot = tiles.at[(sy * NZ + sz) * 2 + half]
        return pltpu.make_async_remote_copy(
            src_ref=slot, dst_ref=slot,
            send_sem=send_sem, recv_sem=recv_sem.at[sem_of.get((half, child), child // NZ)],
            device_id=chip(cy - py, cz - pz), device_id_type=MESH,
        )

    def whole(count, sem):
        spot = tiles.at[pl.ds(0, count)]
        return pltpu.make_async_remote_copy(
            src_ref=spot, dst_ref=spot, send_sem=send_sem, recv_sem=recv_sem.at[sem],
            device_id=chip(0, 1), device_id_type=MESH,
        )

    loads = [
        pltpu.make_async_copy(src, dst, load_sem.at[i])
        for i, (src, dst) in enumerate(
            ((int_ref.at[0, 0], own), (kept_ref, flag), (mask_ref, mask), (amp_ref.at[:, 0], raw))
        )
    ]
    for load in loads:
        load.start()

    hops = set()
    for child, parent in EDGES:
        (cy, cz), (py, pz) = split(child), split(parent)
        hop = ((cy - py) % NY, (cz - pz) % NZ)
        hops |= {hop, (-hop[0] % NY, -hop[1] % NZ)}
    hops = sorted(hops)
    barrier = pltpu.get_barrier_semaphore()
    for hop in hops:
        pl.semaphore_signal(barrier, 1, device_id=chip(*hop), device_id_type=MESH)
    core, at_x, chips = lax.rem(me, 2), lax.div(me, 2), red // 2
    partners = [(pair, me + 1 - 2 * core)] + [(pair, lax.rem(at_x + d, chips) * 2 + core) for d in range(1, chips)]
    for partner in partners:
        pl.semaphore_signal(barrier, 1, device_id=partner, device_id_type=MESH)

    loads[0].wait()
    loads[1].wait()
    kept = flag[0, 0].astype(jnp.float32)
    mine = (own[...].astype(jnp.float32) * kept).astype(jnp.bfloat16)
    tiles[pl.ds(pair * 2, 2)] = mine.reshape(2, width // 2, width)
    pl.semaphore_wait(barrier, len(hops) + len(partners))

    def forward(half, code):
        for child in children.get((half, code), ()):
            copy(half, child, code).start()

    for half in range(2):
        forward(half, 0)

    loads[2].wait()
    loads[3].wait()

    @pl.loop(0, pairs)
    def _(p):
        rows = pl.ds(pl.multiple_of(p * occ, occ), occ)
        for k in range(slabs):
            weight = mask[p, 0, k].astype(jnp.float32).astype(jnp.bfloat16)
            lhs[rows, k * width:(k + 1) * width] = raw[p, k] * weight

    low = occ // red

    def met_copy(g):
        return pltpu.make_async_remote_copy(
            src_ref=part.at[g, 1 - core], dst_ref=met.at[g],
            send_sem=met_send.at[g], recv_sem=met_recv.at[g],
            device_id=(pair, me + 1 - 2 * core), device_id_type=MESH,
        )

    def red_copy(g, d):
        to = lax.rem(at_x + d, chips)
        return pltpu.make_async_remote_copy(
            src_ref=pooled.at[g, to], dst_ref=landed.at[g, at_x],
            send_sem=red_send.at[g, d], recv_sem=red_recv.at[g, d],
            device_id=(pair, to * 2 + core), device_id_type=MESH,
        )

    def multiply(g):
        column, _ = at(-g, 0)
        rhs = jnp.concatenate(
            [tiles[pl.ds((column * NZ + h * slabs) * 2, slabs * 2)].reshape(slabs * width, width) for h in range(2)], axis=1
        )
        total[...] = jnp.dot(lhs[...], rhs, preferred_element_type=jnp.float32)
        for j in range(red):
            rows = [total[p * occ + j * low:p * occ + (j + 1) * low, :] for p in range(pairs)]
            part[g, j % 2, j // 2] = jnp.concatenate(rows, axis=0).astype(jnp.bfloat16)
        met_copy(g).start()

    def pass_on(g):
        met_copy(g).wait_recv()
        pooled[g] = (part[g, core].astype(jnp.float32) + met[g].astype(jnp.float32)).astype(jnp.bfloat16)
        for d in range(1, chips):
            red_copy(g, d).start()

    def finish(g):
        column, _ = at(-g, 0)
        value = part[g, core, at_x].astype(jnp.float32) + met[g, at_x].astype(jnp.float32)
        for d in range(1, chips):
            red_copy(g, d).wait_recv()
            value = value + landed[g, lax.rem(at_x + chips - d, chips)].astype(jnp.float32)
        spot = pl.ds(pl.multiple_of(column * group, group), group)
        out_ref[:, :, spot] = value.reshape(pairs, low, group).astype(jnp.bfloat16)

    for half, code in inner:
        if code:
            copy(half, code, code).wait_recv()
            forward(half, code)
    before = None
    for g in COLUMNS:
        outer = sum(code // NZ == g and (half, code) not in sem_of for half, code in ORDER)
        if outer:
            whole(outer, g).wait_recv()
        multiply(g)
        if before is not None:
            pass_on(before)
        before = g
    finish(COLUMNS[0])
    pass_on(before)
    for g in COLUMNS[1:]:
        finish(g)

    whole(2 * len(EDGES), 0).wait_send()
    for g in range(NY):
        met_copy(g).wait_send()
        for d in range(1, chips):
            red_copy(g, d).wait_send()


def inner_count():
    return len({parent for _, parent in EDGES})


def local(red, amplitudes, integrals, amp_mask, kept_slab_indicator):
    pairs, _, slabs, occ, width = amplitudes.shape
    rows, group = pairs * occ, 2 * width
    out = jax.ShapeDtypeStruct((pairs, occ // red, NY * group), jnp.bfloat16)
    dma = pltpu.SemaphoreType.DMA
    return pl.pallas_call(
        functools.partial(kernel, red),
        out_shape=out,
        in_specs=[
            pl.BlockSpec(memory_space=pltpu.HBM),
            pl.BlockSpec(memory_space=pltpu.HBM),
            pl.BlockSpec(memory_space=pltpu.HBM),
            pl.BlockSpec(memory_space=pltpu.HBM),
        ],
        out_specs=pl.BlockSpec(memory_space=pltpu.VMEM),
        scratch_shapes=[
            pltpu.VMEM((pairs, slabs, occ, width), jnp.bfloat16),
            pltpu.VMEM((rows, slabs * width), jnp.bfloat16),
            pltpu.VMEM((width, width), jnp.bfloat16),
            pltpu.SMEM(amp_mask.shape, jnp.int32),
            pltpu.SMEM(kept_slab_indicator.shape, jnp.int32),
            pltpu.VMEM((NY * NZ * 2, width // 2, width), jnp.bfloat16),
            pltpu.VMEM((rows, group), jnp.float32),
            pltpu.VMEM((NY, 2, red // 2, rows // red, group), jnp.bfloat16),
            pltpu.VMEM((NY, red // 2, rows // red, group), jnp.bfloat16),
            pltpu.VMEM((NY, red // 2, rows // red, group), jnp.bfloat16),
            pltpu.VMEM((NY, red // 2, rows // red, group), jnp.bfloat16),
            dma((4,)), dma, dma((NY + 2 * inner_count(),)),
            dma((NY,)), dma((NY,)), dma((NY, red // 2)), dma((NY, red // 2)),
        ],
        compiler_params=pltpu.CompilerParams(
            collective_id=0, has_side_effects=True, vmem_limit_bytes=63 * 1024 * 1024
        ),
    )(amplitudes, integrals, amp_mask, kept_slab_indicator)


def solution(mesh):
    return jax.shard_map(
        functools.partial(local, mesh.shape["red"]),
        mesh=mesh,
        in_specs=(
            P("pair", "red", None, None, None),
            P("pair", "red", None, None),
            P("pair", "red", None),
            P("pair", "red"),
        ),
        out_specs=P("pair", "red", None),
        check_vma=False,
    )
```

```python
import functools

import jax
import jax.numpy as jnp
from jax import lax
from jax.experimental import pallas as pl
from jax.experimental.pallas import tpu as pltpu
from jax.sharding import PartitionSpec as P

MESH = pl.DeviceIdType.MESH
NY, NZ = 4, 32
EDGES = (
    (2, 0), (25, 0), (3, 2), (9, 2), (4, 3), (18, 25), (121, 25), (5, 4), (24, 25), (11, 9), (32, 0), (122, 121),
    (6, 5), (10, 9), (23, 24), (100, 4), (120, 24), (13, 11), (16, 18), (62, 32), (123, 122), (7, 6), (19, 18),
    (42, 10), (55, 23), (101, 100), (119, 120), (124, 123), (38, 6), (39, 7), (43, 42), (48, 16), (51, 19), (54, 55),
    (61, 62), (63, 32), (96, 0), (102, 101), (107, 11), (109, 13), (112, 16), (118, 119), (92, 124), (1, 2), (8, 9),
    (14, 13), (15, 16), (17, 16), (22, 23), (26, 122), (30, 62), (31, 63), (35, 3), (40, 39), (41, 9), (45, 13),
    (49, 48), (52, 51), (60, 61), (70, 38), (75, 43), (80, 112), (83, 51), (86, 54), (93, 61), (97, 96), (103, 102),
    (108, 107), (110, 109), (115, 19), (117, 118), (64, 0), (66, 2), (90, 92), (12, 13), (20, 19), (21, 22),
    (27, 123), (28, 60), (29, 61), (33, 1), (34, 2), (36, 35), (37, 5), (44, 45), (46, 14), (47, 15), (50, 18),
    (53, 54), (56, 24), (57, 25), (58, 26), (59, 60), (65, 97), (67, 35), (68, 100), (69, 70), (71, 103), (72, 40),
    (73, 41), (74, 75), (76, 108), (77, 109), (78, 110), (79, 80), (81, 49), (82, 83), (84, 52), (85, 117), (87, 86),
    (88, 120), (89, 121), (91, 92), (94, 62), (95, 63), (98, 2), (99, 3), (104, 8), (105, 9), (106, 10), (111, 15),
    (113, 17), (114, 18), (116, 115), (125, 93), (126, 30), (127, 31),
)
ORDER = (
    (0, 32), (1, 96), (0, 96), (1, 32), (0, 2), (1, 30), (0, 64), (1, 64), (0, 63), (1, 97), (0, 97), (1, 63),
    (0, 62), (1, 98), (0, 3), (1, 29), (0, 98), (1, 62), (0, 34), (1, 126), (0, 25), (1, 7), (0, 1), (1, 31), (0, 66),
    (1, 94), (0, 31), (1, 1), (0, 95), (1, 65), (0, 65), (1, 95), (0, 61), (1, 99), (0, 30), (1, 2), (0, 4), (1, 28),
    (0, 94), (1, 66), (0, 35), (1, 125), (0, 24), (1, 8), (0, 99), (1, 61), (0, 121), (1, 39), (0, 57), (1, 103),
    (0, 9), (1, 23), (0, 33), (1, 127), (0, 127), (1, 33), (0, 93), (1, 67), (0, 60), (1, 100), (0, 29), (1, 3),
    (0, 5), (1, 27), (0, 126), (1, 34), (0, 36), (1, 124), (0, 100), (1, 60), (0, 23), (1, 9), (0, 67), (1, 93),
    (0, 122), (1, 38), (0, 120), (1, 40), (0, 56), (1, 104), (0, 18), (1, 14), (0, 10), (1, 22), (0, 89), (1, 71),
    (0, 8), (1, 24), (0, 41), (1, 119), (0, 105), (1, 55), (0, 11), (1, 21), (0, 59), (1, 101), (0, 125), (1, 35),
    (0, 6), (1, 26), (0, 28), (1, 4), (0, 37), (1, 123), (0, 101), (1, 59), (0, 68), (1, 92), (0, 22), (1, 10),
    (0, 55), (1, 105), (0, 123), (1, 37), (0, 26), (1, 6), (0, 119), (1, 41), (0, 88), (1, 72), (0, 114), (1, 46),
    (0, 19), (1, 13), (0, 42), (1, 118), (0, 50), (1, 110), (0, 16), (1, 16), (0, 106), (1, 54), (0, 104), (1, 56),
    (0, 7), (1, 25), (0, 13), (1, 19), (0, 73), (1, 87), (0, 102), (1, 58), (0, 107), (1, 53), (0, 21), (1, 11),
    (0, 38), (1, 122), (0, 54), (1, 106), (0, 27), (1, 5), (0, 124), (1, 36), (0, 58), (1, 102), (0, 118), (1, 42),
    (0, 51), (1, 109), (0, 20), (1, 12), (0, 115), (1, 45), (0, 43), (1, 117), (0, 112), (1, 48), (0, 15), (1, 17),
    (0, 48), (1, 112), (0, 17), (1, 15), (0, 39), (1, 121), (0, 14), (1, 18), (0, 109), (1, 51), (0, 12), (1, 20),
    (0, 45), (1, 115), (0, 103), (1, 57), (0, 70), (1, 90), (0, 108), (1, 52), (0, 86), (1, 74), (0, 53), (1, 107),
    (0, 92), (1, 68), (0, 117), (1, 43), (0, 83), (1, 77), (0, 52), (1, 108), (0, 75), (1, 85), (0, 116), (1, 44),
    (0, 80), (1, 80), (0, 49), (1, 111), (0, 111), (1, 49), (0, 40), (1, 120), (0, 47), (1, 113), (0, 110), (1, 50),
    (0, 113), (1, 47), (0, 44), (1, 116), (0, 46), (1, 114), (0, 69), (1, 91), (0, 77), (1, 83), (0, 87), (1, 73),
    (0, 71), (1, 89), (0, 76), (1, 84), (0, 91), (1, 69), (0, 85), (1, 75), (0, 84), (1, 76), (0, 82), (1, 78),
    (0, 90), (1, 70), (0, 81), (1, 79), (0, 74), (1, 86), (0, 72), (1, 88), (0, 79), (1, 81), (0, 78), (1, 82),
)
COLUMNS = (0, 1, 3, 2)


def split(code):
    return code // NZ, code % NZ


def mirrored(code):
    oy, oz = split(code)
    return (-oy % NY) * NZ + -oz % NZ


def plan():
    children = {}
    for child, parent in EDGES:
        children.setdefault((0, parent), []).append(child)
        children.setdefault((1, mirrored(parent)), []).append(mirrored(child))
    return children


def kernel(
    red, amp_ref, int_ref, mask_ref, kept_ref, out_ref,
    raw, lhs, own, mask, flag, tiles, total, part, met, pooled, landed,
    load_sem, send_sem, recv_sem, met_send, met_recv, red_send, red_recv,
):
    pair, me = lax.axis_index("pair"), lax.axis_index("red")
    y, z = lax.div(pair, NZ), lax.rem(pair, NZ)
    children = plan()
    inner = [node for node in ORDER if node in children]
    sem_of = {node: NY + i for i, node in enumerate(inner)}
    pairs, slabs, occ, width = raw.shape
    group = 2 * width

    def at(oy, oz):
        return lax.rem(y + (oy % NY), NY), lax.rem(z + (oz % NZ), NZ)

    def chip(oy, oz):
        ny, nz = at(oy, oz)
        return (ny * NZ + nz, me)

    def copy(half, child, parent):
        cy, cz = split(child)
        py, pz = split(parent)
        sy, sz = at(-py, -pz)
        slot = tiles.at[(sy * NZ + sz) * 2 + half]
        return pltpu.make_async_remote_copy(
            src_ref=slot, dst_ref=slot,
            send_sem=send_sem, recv_sem=recv_sem.at[sem_of.get((half, child), child // NZ)],
            device_id=chip(cy - py, cz - pz), device_id_type=MESH,
        )

    def whole(count, sem):
        spot = tiles.at[pl.ds(0, count)]
        return pltpu.make_async_remote_copy(
            src_ref=spot, dst_ref=spot, send_sem=send_sem, recv_sem=recv_sem.at[sem],
            device_id=chip(0, 1), device_id_type=MESH,
        )

    loads = [
        pltpu.make_async_copy(src, dst, load_sem.at[i])
        for i, (src, dst) in enumerate(
            ((int_ref.at[0, 0], own), (kept_ref, flag), (mask_ref, mask), (amp_ref.at[:, 0], raw))
        )
    ]
    for load in loads:
        load.start()

    hops = set()
    for child, parent in EDGES:
        (cy, cz), (py, pz) = split(child), split(parent)
        hop = ((cy - py) % NY, (cz - pz) % NZ)
        hops |= {hop, (-hop[0] % NY, -hop[1] % NZ)}
    hops = sorted(hops)
    barrier = pltpu.get_barrier_semaphore()
    for hop in hops:
        pl.semaphore_signal(barrier, 1, device_id=chip(*hop), device_id_type=MESH)
    core, at_x, chips = lax.rem(me, 2), lax.div(me, 2), red // 2
    partners = [(pair, me + 1 - 2 * core)] + [(pair, lax.rem(at_x + d, chips) * 2 + core) for d in range(1, chips)]
    for partner in partners:
        pl.semaphore_signal(barrier, 1, device_id=partner, device_id_type=MESH)

    loads[0].wait()
    loads[1].wait()
    kept = flag[0, 0].astype(jnp.float32)
    mine = (own[...].astype(jnp.float32) * kept).astype(jnp.bfloat16)
    tiles[pl.ds(pair * 2, 2)] = mine.reshape(2, width // 2, width)
    pl.semaphore_wait(barrier, len(hops) + len(partners))

    def forward(half, code):
        for child in children.get((half, code), ()):
            copy(half, child, code).start()

    for half in range(2):
        forward(half, 0)

    loads[2].wait()
    loads[3].wait()

    @pl.loop(0, pairs)
    def _(p):
        rows = pl.ds(pl.multiple_of(p * occ, occ), occ)
        for k in range(slabs):
            weight = mask[p, 0, k].astype(jnp.float32).astype(jnp.bfloat16)
            lhs[rows, k * width:(k + 1) * width] = raw[p, k] * weight

    low = occ // red

    def met_copy(g):
        return pltpu.make_async_remote_copy(
            src_ref=part.at[g, 1 - core], dst_ref=met.at[g],
            send_sem=met_send, recv_sem=met_recv.at[g],
            device_id=(pair, me + 1 - 2 * core), device_id_type=MESH,
        )

    def red_copy(g, d):
        to = lax.rem(at_x + d, chips)
        return pltpu.make_async_remote_copy(
            src_ref=pooled.at[g, to], dst_ref=landed.at[g, at_x],
            send_sem=red_send, recv_sem=red_recv.at[g],
            device_id=(pair, to * 2 + core), device_id_type=MESH,
        )

    def all_of(ref, send, recv):
        return pltpu.make_async_remote_copy(
            src_ref=ref, dst_ref=ref, send_sem=send, recv_sem=recv,
            device_id=partners[0], device_id_type=MESH,
        )

    def multiply(g):
        column, _ = at(-g, 0)
        rhs = jnp.concatenate(
            [tiles[pl.ds((column * NZ + h * slabs) * 2, slabs * 2)].reshape(slabs * width, width) for h in range(2)], axis=1
        )
        total[...] = jnp.dot(lhs[...], rhs, preferred_element_type=jnp.float32)
        for j in range(red):
            rows = [total[p * occ + j * low:p * occ + (j + 1) * low, :] for p in range(pairs)]
            part[g, j % 2, j // 2] = jnp.concatenate(rows, axis=0).astype(jnp.bfloat16)
        met_copy(g).start()

    def pass_on(g):
        met_copy(g).wait_recv()
        pooled[g] = (part[g, core].astype(jnp.float32) + met[g].astype(jnp.float32)).astype(jnp.bfloat16)
        for d in range(1, chips):
            red_copy(g, d).start()

    def finish(g):
        column, _ = at(-g, 0)
        value = part[g, core, at_x].astype(jnp.float32) + met[g, at_x].astype(jnp.float32)
        all_of(landed.at[g, pl.ds(0, chips - 1)], red_send, red_recv.at[g]).wait_recv()
        for d in range(1, chips):
            value = value + landed[g, lax.rem(at_x + chips - d, chips)].astype(jnp.float32)
        spot = pl.ds(pl.multiple_of(column * group, group), group)
        out_ref[:, :, spot] = value.reshape(pairs, low, group).astype(jnp.bfloat16)

    def await_column(g):
        outer = sum(code // NZ == g and (half, code) not in sem_of for half, code in ORDER)
        if outer:
            whole(outer, g).wait_recv()

    for half, code in inner:
        copy(half, code, code).wait_recv()
        forward(half, code)
    first, second, third, last = COLUMNS
    await_column(first)
    multiply(first)
    await_column(second)
    multiply(second)
    pass_on(first)
    await_column(third)
    multiply(third)
    pass_on(second)
    pass_on(third)
    await_column(last)
    multiply(last)
    finish(first)
    pass_on(last)
    for g in (second, third, last):
        finish(g)

    whole(2 * len(EDGES), 0).wait_send()
    all_of(met, met_send, met_recv.at[0]).wait_send()
    all_of(landed.at[:, pl.ds(0, chips - 1)], red_send, red_recv.at[0]).wait_send()


def inner_count():
    return len({parent for _, parent in EDGES if parent})


def local(red, amplitudes, integrals, amp_mask, kept_slab_indicator):
    pairs, _, slabs, occ, width = amplitudes.shape
    rows, group = pairs * occ, 2 * width
    out = jax.ShapeDtypeStruct((pairs, occ // red, NY * group), jnp.bfloat16)
    dma = pltpu.SemaphoreType.DMA
    return pl.pallas_call(
        functools.partial(kernel, red),
        out_shape=out,
        in_specs=[
            pl.BlockSpec(memory_space=pltpu.HBM),
            pl.BlockSpec(memory_space=pltpu.HBM),
            pl.BlockSpec(memory_space=pltpu.HBM),
            pl.BlockSpec(memory_space=pltpu.HBM),
        ],
        out_specs=pl.BlockSpec(memory_space=pltpu.VMEM),
        scratch_shapes=[
            pltpu.VMEM((pairs, slabs, occ, width), jnp.bfloat16),
            pltpu.VMEM((rows, slabs * width), jnp.bfloat16),
            pltpu.VMEM((width, width), jnp.bfloat16),
            pltpu.SMEM(amp_mask.shape, jnp.int32),
            pltpu.SMEM(kept_slab_indicator.shape, jnp.int32),
            pltpu.VMEM((NY * NZ * 2, width // 2, width), jnp.bfloat16),
            pltpu.VMEM((rows, group), jnp.float32),
            pltpu.VMEM((NY, 2, red // 2, rows // red, group), jnp.bfloat16),
            pltpu.VMEM((NY, red // 2, rows // red, group), jnp.bfloat16),
            pltpu.VMEM((NY, red // 2, rows // red, group), jnp.bfloat16),
            pltpu.VMEM((NY, red // 2, rows // red, group), jnp.bfloat16),
            dma((4,)), dma, dma((NY + 2 * inner_count(),)),
            dma, dma((NY,)), dma, dma((NY,)),
        ],
        compiler_params=pltpu.CompilerParams(
            collective_id=0, has_side_effects=True, vmem_limit_bytes=63 * 1024 * 1024
        ),
    )(amplitudes, integrals, amp_mask, kept_slab_indicator)


def solution(mesh):
    return jax.shard_map(
        functools.partial(local, mesh.shape["red"]),
        mesh=mesh,
        in_specs=(
            P("pair", "red", None, None, None),
            P("pair", "red", None, None),
            P("pair", "red", None),
            P("pair", "red"),
        ),
        out_specs=P("pair", "red", None),
        check_vma=False,
    )
```

```python
import functools

import jax
import jax.numpy as jnp
from jax import lax
from jax.experimental import pallas as pl
from jax.experimental.pallas import tpu as pltpu
from jax.sharding import PartitionSpec as P

MESH = pl.DeviceIdType.MESH
NY, NZ = 4, 32
EDGES = (
    (2, 0), (25, 0), (3, 2), (9, 2), (4, 3), (18, 25), (121, 25), (5, 4), (24, 25), (11, 9), (32, 0), (122, 121),
    (6, 5), (10, 9), (23, 24), (100, 4), (120, 24), (13, 11), (16, 18), (62, 32), (123, 122), (7, 6), (19, 18),
    (42, 10), (55, 23), (101, 100), (119, 120), (124, 123), (38, 6), (39, 7), (43, 42), (48, 16), (51, 19), (54, 55),
    (61, 62), (63, 32), (96, 0), (102, 101), (107, 11), (109, 13), (112, 16), (118, 119), (92, 124), (1, 2), (8, 9),
    (14, 13), (15, 16), (17, 16), (22, 23), (26, 122), (30, 62), (31, 63), (35, 3), (40, 39), (41, 9), (45, 13),
    (49, 48), (52, 51), (60, 61), (70, 38), (75, 43), (80, 112), (83, 51), (86, 54), (93, 61), (97, 96), (103, 102),
    (108, 107), (110, 109), (115, 19), (117, 118), (64, 0), (66, 2), (90, 92), (12, 13), (20, 19), (21, 22),
    (27, 123), (28, 60), (29, 61), (33, 1), (34, 2), (36, 35), (37, 5), (44, 45), (46, 14), (47, 15), (50, 18),
    (53, 54), (56, 24), (57, 25), (58, 26), (59, 60), (65, 97), (67, 35), (68, 100), (69, 70), (71, 103), (72, 40),
    (73, 41), (74, 75), (76, 108), (77, 109), (78, 110), (79, 80), (81, 49), (82, 83), (84, 52), (85, 117), (87, 86),
    (88, 120), (89, 121), (91, 92), (94, 62), (95, 63), (98, 2), (99, 3), (104, 8), (105, 9), (106, 10), (111, 15),
    (113, 17), (114, 18), (116, 115), (125, 93), (126, 30), (127, 31),
)
ORDER = (
    (0, 32), (1, 96), (0, 96), (1, 32), (0, 2), (1, 30), (0, 64), (1, 64), (0, 63), (1, 97), (0, 97), (1, 63),
    (0, 62), (1, 98), (0, 3), (1, 29), (0, 98), (1, 62), (0, 34), (1, 126), (0, 25), (1, 7), (0, 1), (1, 31), (0, 66),
    (1, 94), (0, 31), (1, 1), (0, 95), (1, 65), (0, 65), (1, 95), (0, 61), (1, 99), (0, 30), (1, 2), (0, 4), (1, 28),
    (0, 94), (1, 66), (0, 35), (1, 125), (0, 24), (1, 8), (0, 99), (1, 61), (0, 121), (1, 39), (0, 57), (1, 103),
    (0, 9), (1, 23), (0, 33), (1, 127), (0, 127), (1, 33), (0, 93), (1, 67), (0, 60), (1, 100), (0, 29), (1, 3),
    (0, 5), (1, 27), (0, 126), (1, 34), (0, 36), (1, 124), (0, 100), (1, 60), (0, 23), (1, 9), (0, 67), (1, 93),
    (0, 122), (1, 38), (0, 120), (1, 40), (0, 56), (1, 104), (0, 18), (1, 14), (0, 10), (1, 22), (0, 89), (1, 71),
    (0, 8), (1, 24), (0, 41), (1, 119), (0, 105), (1, 55), (0, 11), (1, 21), (0, 59), (1, 101), (0, 125), (1, 35),
    (0, 6), (1, 26), (0, 28), (1, 4), (0, 37), (1, 123), (0, 101), (1, 59), (0, 68), (1, 92), (0, 22), (1, 10),
    (0, 55), (1, 105), (0, 123), (1, 37), (0, 26), (1, 6), (0, 119), (1, 41), (0, 88), (1, 72), (0, 114), (1, 46),
    (0, 19), (1, 13), (0, 42), (1, 118), (0, 50), (1, 110), (0, 16), (1, 16), (0, 106), (1, 54), (0, 104), (1, 56),
    (0, 7), (1, 25), (0, 13), (1, 19), (0, 73), (1, 87), (0, 102), (1, 58), (0, 107), (1, 53), (0, 21), (1, 11),
    (0, 38), (1, 122), (0, 54), (1, 106), (0, 27), (1, 5), (0, 124), (1, 36), (0, 58), (1, 102), (0, 118), (1, 42),
    (0, 51), (1, 109), (0, 20), (1, 12), (0, 115), (1, 45), (0, 43), (1, 117), (0, 112), (1, 48), (0, 15), (1, 17),
    (0, 48), (1, 112), (0, 17), (1, 15), (0, 39), (1, 121), (0, 14), (1, 18), (0, 109), (1, 51), (0, 12), (1, 20),
    (0, 45), (1, 115), (0, 103), (1, 57), (0, 70), (1, 90), (0, 108), (1, 52), (0, 86), (1, 74), (0, 53), (1, 107),
    (0, 92), (1, 68), (0, 117), (1, 43), (0, 83), (1, 77), (0, 52), (1, 108), (0, 75), (1, 85), (0, 116), (1, 44),
    (0, 80), (1, 80), (0, 49), (1, 111), (0, 111), (1, 49), (0, 40), (1, 120), (0, 47), (1, 113), (0, 110), (1, 50),
    (0, 113), (1, 47), (0, 44), (1, 116), (0, 46), (1, 114), (0, 69), (1, 91), (0, 77), (1, 83), (0, 87), (1, 73),
    (0, 71), (1, 89), (0, 76), (1, 84), (0, 91), (1, 69), (0, 85), (1, 75), (0, 84), (1, 76), (0, 82), (1, 78),
    (0, 90), (1, 70), (0, 81), (1, 79), (0, 74), (1, 86), (0, 72), (1, 88), (0, 79), (1, 81), (0, 78), (1, 82),
)
COLUMNS = (0, 1, 3, 2)


def split(code):
    return code // NZ, code % NZ


def mirrored(code):
    oy, oz = split(code)
    return (-oy % NY) * NZ + -oz % NZ


def plan():
    children = {}
    for child, parent in EDGES:
        children.setdefault((0, parent), []).append(child)
        children.setdefault((1, mirrored(parent)), []).append(mirrored(child))
    return children


def kernel(
    red, amp_ref, int_ref, mask_ref, kept_ref, out_ref,
    raw, lhs, own, mask, flag, tiles, total, part, met, pooled, landed,
    load_sem, send_sem, recv_sem, met_send, met_recv, red_send, red_recv,
):
    pair, me = lax.axis_index("pair"), lax.axis_index("red")
    y, z = lax.div(pair, NZ), lax.rem(pair, NZ)
    children = plan()
    inner = [node for node in ORDER if node in children]
    sem_of = {node: NY + i for i, node in enumerate(inner)}
    pairs, slabs, occ, width = raw.shape
    group = 2 * width

    def at(oy, oz):
        return lax.rem(y + (oy % NY), NY), lax.rem(z + (oz % NZ), NZ)

    def chip(oy, oz):
        ny, nz = at(oy, oz)
        return (ny * NZ + nz, me)

    def copy(half, child, parent):
        cy, cz = split(child)
        py, pz = split(parent)
        sy, sz = at(-py, -pz)
        slot = tiles.at[(sy * NZ + sz) * 2 + half]
        return pltpu.make_async_remote_copy(
            src_ref=slot, dst_ref=slot,
            send_sem=send_sem, recv_sem=recv_sem.at[sem_of.get((half, child), child // NZ)],
            device_id=chip(cy - py, cz - pz), device_id_type=MESH,
        )

    def whole(count, sem):
        spot = tiles.at[pl.ds(0, count)]
        return pltpu.make_async_remote_copy(
            src_ref=spot, dst_ref=spot, send_sem=send_sem, recv_sem=recv_sem.at[sem],
            device_id=chip(0, 1), device_id_type=MESH,
        )

    hops = set()
    for child, parent in EDGES:
        (cy, cz), (py, pz) = split(child), split(parent)
        hop = ((cy - py) % NY, (cz - pz) % NZ)
        hops |= {hop, (-hop[0] % NY, -hop[1] % NZ)}
    hops = sorted(hops, key=lambda hop: (-min(hop[1], NZ - hop[1]), hop))
    barrier = pltpu.get_barrier_semaphore()
    for hop in hops:
        pl.semaphore_signal(barrier, 1, device_id=chip(*hop), device_id_type=MESH)
    core, at_x, chips = lax.rem(me, 2), lax.div(me, 2), red // 2
    partners = [(pair, me + 1 - 2 * core)] + [(pair, lax.rem(at_x + d, chips) * 2 + core) for d in range(1, chips)]
    for partner in partners:
        pl.semaphore_signal(barrier, 1, device_id=partner, device_id_type=MESH)

    loads = [
        pltpu.make_async_copy(src, dst, load_sem.at[i])
        for i, (src, dst) in enumerate(
            ((int_ref.at[0, 0], own), (kept_ref, flag), (mask_ref, mask), (amp_ref.at[:, 0], raw))
        )
    ]
    for load in loads:
        load.start()

    loads[0].wait()
    loads[1].wait()
    kept = flag[0, 0].astype(jnp.float32)
    mine = (own[...].astype(jnp.float32) * kept).astype(jnp.bfloat16)
    tiles[pl.ds(pair * 2, 2)] = mine.reshape(2, width // 2, width)
    pl.semaphore_wait(barrier, len(hops) + len(partners))

    def forward(half, code):
        for child in children.get((half, code), ()):
            copy(half, child, code).start()

    for half in range(2):
        forward(half, 0)

    loads[2].wait()
    loads[3].wait()

    @pl.loop(0, pairs)
    def _(p):
        rows = pl.ds(pl.multiple_of(p * occ, occ), occ)
        for k in range(slabs):
            weight = mask[p, 0, k].astype(jnp.float32).astype(jnp.bfloat16)
            lhs[rows, k * width:(k + 1) * width] = raw[p, k] * weight

    low = occ // red

    def met_copy(g):
        return pltpu.make_async_remote_copy(
            src_ref=part.at[g, 1 - core], dst_ref=met.at[g],
            send_sem=met_send, recv_sem=met_recv.at[g],
            device_id=(pair, me + 1 - 2 * core), device_id_type=MESH,
        )

    def red_copy(g, d):
        to = lax.rem(at_x + d, chips)
        return pltpu.make_async_remote_copy(
            src_ref=pooled.at[g, to], dst_ref=landed.at[g, at_x],
            send_sem=red_send, recv_sem=red_recv.at[g],
            device_id=(pair, to * 2 + core), device_id_type=MESH,
        )

    def all_of(ref, send, recv):
        return pltpu.make_async_remote_copy(
            src_ref=ref, dst_ref=ref, send_sem=send, recv_sem=recv,
            device_id=partners[0], device_id_type=MESH,
        )

    def multiply(g):
        column, _ = at(-g, 0)
        rhs = jnp.concatenate(
            [tiles[pl.ds((column * NZ + h * slabs) * 2, slabs * 2)].reshape(slabs * width, width) for h in range(2)], axis=1
        )
        total[...] = jnp.dot(lhs[...], rhs, preferred_element_type=jnp.float32)
        for j in range(red):
            rows = [total[p * occ + j * low:p * occ + (j + 1) * low, :] for p in range(pairs)]
            part[g, j % 2, j // 2] = jnp.concatenate(rows, axis=0).astype(jnp.bfloat16)
        met_copy(g).start()

    def pass_on(g):
        met_copy(g).wait_recv()
        pooled[g] = (part[g, core].astype(jnp.float32) + met[g].astype(jnp.float32)).astype(jnp.bfloat16)
        for d in sorted(range(1, chips), key=lambda d: -min(d, chips - d)):
            red_copy(g, d).start()

    def finish(g):
        column, _ = at(-g, 0)
        value = part[g, core, at_x].astype(jnp.float32) + met[g, at_x].astype(jnp.float32)
        all_of(landed.at[g, pl.ds(0, chips - 1)], red_send, red_recv.at[g]).wait_recv()
        for d in range(1, chips):
            value = value + landed[g, lax.rem(at_x + chips - d, chips)].astype(jnp.float32)
        spot = pl.ds(pl.multiple_of(column * group, group), group)
        out_ref[:, :, spot] = value.reshape(pairs, low, group).astype(jnp.bfloat16)

    def await_column(g):
        outer = sum(code // NZ == g and (half, code) not in sem_of for half, code in ORDER)
        if outer:
            whole(outer, g).wait_recv()

    for half, code in inner:
        copy(half, code, code).wait_recv()
        forward(half, code)
    first, second, third, last = COLUMNS
    await_column(first)
    multiply(first)
    await_column(second)
    multiply(second)
    pass_on(first)
    await_column(third)
    multiply(third)
    pass_on(second)
    pass_on(third)
    await_column(last)
    multiply(last)
    finish(first)
    pass_on(last)
    for g in (second, third, last):
        finish(g)

    whole(2 * len(EDGES), 0).wait_send()
    all_of(met, met_send, met_recv.at[0]).wait_send()
    all_of(landed.at[:, pl.ds(0, chips - 1)], red_send, red_recv.at[0]).wait_send()


def inner_count():
    return len({parent for _, parent in EDGES if parent})


def local(red, amplitudes, integrals, amp_mask, kept_slab_indicator):
    pairs, _, slabs, occ, width = amplitudes.shape
    rows, group = pairs * occ, 2 * width
    out = jax.ShapeDtypeStruct((pairs, occ // red, NY * group), jnp.bfloat16)
    dma = pltpu.SemaphoreType.DMA
    return pl.pallas_call(
        functools.partial(kernel, red),
        out_shape=out,
        in_specs=[
            pl.BlockSpec(memory_space=pltpu.HBM),
            pl.BlockSpec(memory_space=pltpu.HBM),
            pl.BlockSpec(memory_space=pltpu.HBM),
            pl.BlockSpec(memory_space=pltpu.HBM),
        ],
        out_specs=pl.BlockSpec(memory_space=pltpu.VMEM),
        scratch_shapes=[
            pltpu.VMEM((pairs, slabs, occ, width), jnp.bfloat16),
            pltpu.VMEM((rows, slabs * width), jnp.bfloat16),
            pltpu.VMEM((width, width), jnp.bfloat16),
            pltpu.SMEM(amp_mask.shape, jnp.int32),
            pltpu.SMEM(kept_slab_indicator.shape, jnp.int32),
            pltpu.VMEM((NY * NZ * 2, width // 2, width), jnp.bfloat16),
            pltpu.VMEM((rows, group), jnp.float32),
            pltpu.VMEM((NY, 2, red // 2, rows // red, group), jnp.bfloat16),
            pltpu.VMEM((NY, red // 2, rows // red, group), jnp.bfloat16),
            pltpu.VMEM((NY, red // 2, rows // red, group), jnp.bfloat16),
            pltpu.VMEM((NY, red // 2, rows // red, group), jnp.bfloat16),
            dma((4,)), dma, dma((NY + 2 * inner_count(),)),
            dma, dma((NY,)), dma, dma((NY,)),
        ],
        compiler_params=pltpu.CompilerParams(
            collective_id=0, has_side_effects=True, vmem_limit_bytes=63 * 1024 * 1024
        ),
    )(amplitudes, integrals, amp_mask, kept_slab_indicator)


def solution(mesh):
    return jax.shard_map(
        functools.partial(local, mesh.shape["red"]),
        mesh=mesh,
        in_specs=(
            P("pair", "red", None, None, None),
            P("pair", "red", None, None),
            P("pair", "red", None),
            P("pair", "red"),
        ),
        out_specs=P("pair", "red", None),
        check_vma=False,
    )
```
